32 devices in a mesh: order: 4 (over y, x), level: 4 (over z), freq: 2 (over core).
Axes of the slice: x: 2, y: 2, z: 4, core: 2. Of those that a mesh axis runs over, the one named last changes fastest.
Arguments:
- fourier: bfloat16 [16, 16, 4, 128, 512], P('freq', None, 'level', 'order'), parts along dimension 0, may hold values from -6 to 6
- order_slot: int32 [8], replicated, may hold values from 0 to 7, each once
- coeff_self: bfloat16 [6, 8, 64, 128, 128], P(None, 'order', 'level'), may hold values from -0.375 to 0.375
- coeff_pair: bfloat16 [6, 8, 64, 128, 128], P(None, 'order', 'level'), may hold values from -0.375 to 0.375
Outputs:
- butterfly: bfloat16 [16, 64, 128, 512], P(('freq', 'order'), 'level'), parts along dimension 0
The draws below stay inside these ranges and needn't reach their ends.
There are 2 independent parts, one for each index of `freq`. The reference program is written for one: setup_inputs(seed, part) draws one part's arguments, and reference() takes and returns one part's arrays. A program takes and returns all parts, laid end to end along the dimension named above; an argument that names none is the same for every part. Nothing has to cross between parts.
Inputs may be any that keep to these rules, and one draw needn't show every extreme that they name: order_slot is a permutation of the orders.
All inputs are finite; a program needn't handle non-finite values.
Results may differ from the reference program's by a relative error of at most 0.008.
Values may be sent and summed in bfloat16 or wider, within the bound.
No kernel may reach another device: no remote copies, remote signals or barrier semaphores. Data moves between devices by JAX's collectives and lax.ppermute only.
A program may use at most 64 MiB of HBM per device.

```python
import jax
import jax.numpy as jnp

ROWS = 128
FIELDS = 256
LEAVES = 64
LEVELS = 6
BLK_DEV = 16
ORDERS = 8
N_LEVEL = 4


def level_of(key, shape, shards, low, top_value):
    def one(axis_at, blocks):
        draws = jax.random.uniform(jax.random.fold_in(jax.random.fold_in(key, 6), axis_at), (blocks,), jnp.float32, low / len(shards), top_value / len(shards))
        return jnp.repeat(jnp.exp(draws), shape[axis_at] // blocks).reshape((-1,) + (1,) * (len(shape) - axis_at - 1))

    level = one(*shards[0])
    for cut in shards[1:]:
        level = level * one(*cut)
    return level


def noise(stream_key, dims, spread, bound, cuts=(), kind=jnp.bfloat16):
    drawn = spread * jax.random.normal(stream_key, dims, jnp.float32)
    if cuts:
        drawn = drawn * level_of(stream_key, dims, cuts, -0.22, 0.18)
    return jnp.clip(drawn, -bound, bound).astype(kind)


def setup_inputs(seed: int = 0, part: int = 0) -> dict:
    arg_keys = jax.random.split(jax.random.key(seed), 5)
    own_keys = jax.random.split(jax.random.fold_in(arg_keys[4], part), 5)
    return {
        "fourier": noise(own_keys[0], (ORDERS, BLK_DEV, N_LEVEL, ROWS, 2 * FIELDS), 1.0, 6.0, ((2, 4), (3, 4))),
        "order_slot": jax.random.permutation(arg_keys[1], ORDERS).astype(jnp.int32),
        "coeff_self": noise(arg_keys[2], (LEVELS, ORDERS, LEAVES, ROWS, ROWS), (2 * ROWS) ** -0.5, 0.375, ((1, 4), (2, 4))),
        "coeff_pair": noise(arg_keys[3], (LEVELS, ORDERS, LEAVES, ROWS, ROWS), (2 * ROWS) ** -0.5, 0.375, ((1, 4), (2, 4))),
    }


def partner_blocks(values, height):
    extent = values.shape
    halves = values.reshape(extent[0], extent[1] >> (height + 1), 2, 1 << height, extent[2], extent[3])
    return halves[:, :, ::-1].reshape(extent)


def reference(fourier, order_slot, coeff_self, coeff_pair):
    current = jnp.take(fourier, order_slot.astype(jnp.int32), axis=0)
    current = current.reshape(ORDERS, LEAVES, ROWS, 2 * FIELDS)
    for height in range(LEVELS):
        partner = partner_blocks(current, height)
        mixed_sum = jnp.einsum("sbrq,sbqc->sbrc", coeff_self[height].astype(jnp.float32), current.astype(jnp.float32))
        mixed_sum = mixed_sum + jnp.einsum("sbrq,sbqc->sbrc", coeff_pair[height].astype(jnp.float32), partner.astype(jnp.float32))
        current = mixed_sum.astype(jnp.bfloat16)
    return current
```

```python
import functools

import jax
import jax.numpy as jnp
from jax import lax
from jax.experimental import pallas as pl
from jax.experimental.pallas import tpu as pltpu
from jax.sharding import PartitionSpec as P

COLUMN_PARTS = 2
VMEM = 48 * 1024 * 1024


def params(steps):
    return pltpu.CompilerParams(
        dimension_semantics=("arbitrary",) * steps, vmem_limit_bytes=VMEM
    )


def cost(flops, moved):
    return pl.CostEstimate(flops=flops, bytes_accessed=moved, transcendentals=0)


def swap(value, axis, mask):
    pairs = [(source, source ^ mask) for source in range(lax.axis_size(axis))]
    return lax.ppermute(value, axis, pairs)


def take_kernel(place_ref, slot_ref, *refs):
    half = len(refs) // 2
    for source, target in zip(refs[:half], refs[half:]):
        target[...] = source[...].reshape(target.shape)


def take_rows(fourier, place, order_slot, slot, part, masks, order_count, width):
    orders, blocks, _, rows, _ = fourier.shape
    slots_here = order_slot.shape[0] // order_count
    level_count = lax.axis_size("level")
    group = blocks // level_count
    block = (1, group, 1, rows, width)

    def source_map(mask, order, place, slots):
        return (slots[order * slots_here + slot], place[0] ^ mask, 0, 0, part)

    return pl.pallas_call(
        take_kernel,
        grid_spec=pltpu.PrefetchScalarGridSpec(
            num_scalar_prefetch=2,
            grid=(order_count,),
            in_specs=[pl.BlockSpec(block, functools.partial(source_map, mask)) for mask in masks],
            out_specs=[
                pl.BlockSpec((1, group, rows, width), lambda order, place, slots: (order, 0, 0, 0))
                for _ in masks
            ],
        ),
        out_shape=[
            jax.ShapeDtypeStruct((order_count, group, rows, width), fourier.dtype) for _ in masks
        ],
        compiler_params=params(1),
        cost_estimate=cost(0, 4 * len(masks) * order_count * group * rows * width),
        name="take_rows",
    )(place, order_slot, *[fourier] * len(masks))


def gather_kernel(masks, place_ref, slot_ref, own_ref, *refs):
    target = refs[-1]
    for mask, source in zip(masks, (own_ref,) + refs[:-1]):
        at = place_ref[0] ^ mask
        target[0, :, pl.ds(at, 1)] = source[...].reshape(target[0, :, pl.ds(0, 1)].shape)


def gather_blocks(fourier, received, place, order_slot, slot, part, order_count, width):
    _, blocks, _, rows, _ = fourier.shape
    slots_here = order_slot.shape[0] // order_count
    level_count = lax.axis_size("level")
    group = blocks // level_count

    def own_map(order, place, slots):
        return (slots[order * slots_here + slot], place[0], 0, 0, part)

    return pl.pallas_call(
        functools.partial(gather_kernel, tuple(range(level_count))),
        grid_spec=pltpu.PrefetchScalarGridSpec(
            num_scalar_prefetch=2,
            grid=(order_count,),
            in_specs=[pl.BlockSpec((1, group, 1, rows, width), own_map)]
            + [
                pl.BlockSpec((1, group, rows, width), lambda order, place, slots: (order, 0, 0, 0))
                for _ in received
            ],
            out_specs=pl.BlockSpec(
                (1, group, level_count, rows, width), lambda order, place, slots: (order, 0, 0, 0, 0)
            ),
        ),
        out_shape=jax.ShapeDtypeStruct(
            (order_count, group, level_count, rows, width), fourier.dtype
        ),
        compiler_params=params(1),
        cost_estimate=cost(0, 4 * order_count * blocks * rows * width),
        name="gather_blocks",
    )(place, order_slot, fourier, *received)


def low_kernel(rows_ref, self_ref, pair_ref, out_ref, state):
    level = pl.program_id(0)
    levels = pl.num_programs(0)
    groups, blocks, rows, width = rows_ref.shape
    bits = blocks.bit_length() - 1

    def block_of(height, block):
        if height == 0:
            return [rows_ref[group, block] for group in range(groups)]
        return [state[block]]

    for height in range(bits):

        @pl.when(level == height)
        def _(height=height):
            target = out_ref if height == bits - 1 else state
            for low in range(blocks):
                high = low ^ (1 << height)
                if high < low:
                    continue
                values = jnp.concatenate(block_of(height, low) + block_of(height, high), axis=0)
                factors = jnp.concatenate(
                    [
                        jnp.concatenate([self_ref[0, 0, low], pair_ref[0, 0, low]], axis=1),
                        jnp.concatenate([pair_ref[0, 0, high], self_ref[0, 0, high]], axis=1),
                    ],
                    axis=0,
                )
                mixed = jnp.dot(factors, values, preferred_element_type=jnp.float32)
                mixed = mixed.astype(target.dtype)
                target[low] = mixed[: mixed.shape[0] // 2]
                target[high] = mixed[mixed.shape[0] // 2 :]


def low_levels(rows, coeff_self, coeff_pair, slot):
    groups, blocks, height, width = rows.shape
    cycle = coeff_self.shape[3]
    bits = blocks.bit_length() - 1
    factor = pl.BlockSpec((1, 1, blocks, cycle, cycle), lambda level: (level, slot, 0, 0, 0))
    return pl.pallas_call(
        low_kernel,
        grid=(bits,),
        in_specs=[
            pl.BlockSpec((groups, blocks, height, width), lambda level: (0, 0, 0, 0)),
            factor,
            factor,
        ],
        out_specs=pl.BlockSpec((blocks, cycle, width), lambda level: (0, 0, 0)),
        out_shape=jax.ShapeDtypeStruct((blocks, cycle, width), rows.dtype),
        scratch_shapes=[pltpu.VMEM((blocks, cycle, width), rows.dtype)],
        compiler_params=params(1),
        cost_estimate=cost(
            4 * bits * blocks * cycle * cycle * width,
            4 * blocks * cycle * width + 4 * bits * blocks * cycle * cycle,
        ),
        name="low_levels",
    )(rows, coeff_self, coeff_pair)


def high_kernel(own_ref, other_ref, self_ref, pair_ref, *refs):
    target = refs[-1]
    lead = len(target.shape) - 3
    for block in range(own_ref.shape[0]):
        factors = jnp.concatenate([self_ref[0, 0, block], pair_ref[0, 0, block]], axis=1)
        values = jnp.concatenate([own_ref[block], other_ref[block]], axis=0)
        mixed = jnp.dot(factors, values, preferred_element_type=jnp.float32)
        target[(0,) * lead + (block,)] = mixed.astype(target.dtype)


def high_level(own, other, coeff_self, coeff_pair, level, slot, final=None):
    blocks, cycle, width = own.shape
    step = min(4, blocks)
    value = pl.BlockSpec((step, cycle, width), lambda at: (at, 0, 0))
    factor = pl.BlockSpec((1, 1, step, cycle, cycle), lambda at: (level, slot, at, 0, 0))
    operands = [own, other, coeff_self, coeff_pair]
    in_specs = [value, value, factor, factor]
    aliases = {}
    if final is None:
        out_spec, out_shape = value, jax.ShapeDtypeStruct(own.shape, own.dtype)
    else:
        result, shape, part = final
        out_spec = pl.BlockSpec((1, step, cycle, width), lambda at: (slot, at, 0, part))
        out_shape = jax.ShapeDtypeStruct(shape, own.dtype)
        if result is not None:
            operands.append(result)
            in_specs.append(pl.BlockSpec(memory_space=pl.ANY))
            aliases = {4: 0}
    return pl.pallas_call(
        high_kernel,
        grid=(blocks // step,),
        in_specs=in_specs,
        out_specs=out_spec,
        out_shape=out_shape,
        input_output_aliases=aliases,
        compiler_params=params(1),
        cost_estimate=cost(
            4 * blocks * cycle * cycle * width,
            6 * blocks * cycle * width + 4 * blocks * cycle * cycle,
        ),
        name="high_level",
    )(*operands)


def local(fourier, order_slot, coeff_self, coeff_pair):
    order_count = lax.axis_size("order")
    level_count = lax.axis_size("level")
    levels, orders_here, blocks_here, cycle_rows, _ = coeff_self.shape
    rows_here, columns = fourier.shape[3:]
    local_bits = blocks_here.bit_length() - 1
    width = columns // COLUMN_PARTS
    place = lax.axis_index("level").astype(jnp.int32).reshape(1)
    chunks = [(slot, part) for slot in range(orders_here) for part in range(COLUMN_PARTS)]
    masks = tuple(range(1, level_count))

    current = []
    for slot, part in chunks:
        outgoing = take_rows(
            fourier, place, order_slot, slot, part, masks, order_count, width
        )
        received = [swap(value, "level", mask) for value, mask in zip(outgoing, masks)]
        blocks = gather_blocks(
            fourier, received, place, order_slot, slot, part, order_count, width
        )
        blocks = blocks.reshape(order_count, blocks_here, rows_here, width)
        rows = lax.all_to_all(blocks, "order", split_axis=0, concat_axis=0, tiled=True)
        if rows_here % 16:
            rows = rows.transpose(1, 0, 2, 3).reshape(1, blocks_here, cycle_rows, width)
        current.append(low_levels(rows, coeff_self, coeff_pair, slot))

    result = None
    shape = (orders_here, blocks_here, cycle_rows, columns)
    for (slot, part), value in zip(chunks, current):
        for level in range(local_bits, levels):
            other = swap(value, "level", 1 << (level - local_bits))
            final = (result, shape, part) if level == levels - 1 else None
            value = high_level(value, other, coeff_self, coeff_pair, level, slot, final)
        result = value
    return result


def solution(mesh):
    placed = (
        P("freq", None, "level", "order", None),
        P(),
        P(None, "order", "level", None, None),
        P(None, "order", "level", None, None),
    )
    return jax.shard_map(
        local,
        mesh=mesh,
        in_specs=placed,
        out_specs=P(("freq", "order"), "level", None, None),
        check_vma=False,
    )
```

```python
import functools

import jax
import jax.numpy as jnp
from jax import lax
from jax.experimental import pallas as pl
from jax.experimental.pallas import tpu as pltpu
from jax.sharding import PartitionSpec as P

VMEM = 48 * 1024 * 1024
COLUMN_PARTS = 2
TAKE, GATHER, LOW = "take", "gather", "low"
DIRECT, MIXED, PAIRS = "direct", "mixed", "pairs"
MODES = (DIRECT, DIRECT, DIRECT, MIXED,)
ORDER = (
    (TAKE, 0), (TAKE, 1), (LOW, 0), (TAKE, 2), (1, 0), (TAKE, 3), (LOW, 1), (1, 1), (LOW, 2),
    (GATHER, 3), (2, 0), (1, 2), (LOW, 3), (2, 1), (1, 3), (2, 2), (2, 3),
)


def run_order(count, steps, pairs):
    if count == len(MODES) and steps == 2 and pairs:
        return MODES, ORDER
    order = []
    for turn in range(count + steps + 2):
        jobs = [(TAKE, turn), (LOW, turn - 1)]
        jobs += [(step, turn - 1 - step) for step in range(1, steps + 1)]
        order += [job for job in jobs if 0 <= job[1] < count]
    return (DIRECT,) * count, order


def params(steps):
    return pltpu.CompilerParams(
        dimension_semantics=("arbitrary",) * steps, vmem_limit_bytes=VMEM
    )


def cost():
    return pl.CostEstimate(flops=0, bytes_accessed=1024, transcendentals=0)


def anywhere(values):
    return [pl.BlockSpec(memory_space=pl.ANY)] * len(values)


def swap(value, axis, mask):
    pairs = [(source, source ^ mask) for source in range(lax.axis_size(axis))]
    return lax.ppermute(value, axis, pairs)


def copy_kernel(count, level_ref, order_ref, slot_ref, *refs):
    for source, target in zip(refs[:count], refs[-count:]):
        target[...] = source[...].reshape(target.shape)


def take_rows(fourier, places, chunk, masks, order_count, after):
    slot, start, width = chunk
    _, blocks, _, rows, _ = fourier.shape
    slots_here = places[2].shape[0] // order_count
    group = blocks // lax.axis_size("level") if masks else blocks

    def source_map(mask, order, level, coordinate, slots):
        part = level[0] ^ mask if masks else 0
        return (slots[order * slots_here + slot], part, 0, 0, start // width)

    shape = (order_count, group, rows, width)
    return pl.pallas_call(
        functools.partial(copy_kernel, len(masks) or 1),
        grid_spec=pltpu.PrefetchScalarGridSpec(
            num_scalar_prefetch=3,
            grid=(order_count,),
            in_specs=[
                pl.BlockSpec((1, group, 1, rows, width), functools.partial(source_map, mask))
                for mask in masks or (0,)
            ]
            + anywhere(after),
            out_specs=[
                pl.BlockSpec((1,) + shape[1:], lambda order, *places: (order, 0, 0, 0))
                for _ in masks or (0,)
            ],
        ),
        out_shape=[jax.ShapeDtypeStruct(shape, fourier.dtype) for _ in masks or (0,)],
        compiler_params=params(1),
        cost_estimate=cost(),
        name="take_rows",
    )(*places, *[fourier] * (len(masks) or 1), *after)


def gather_kernel(sources, targets, level_ref, order_ref, slot_ref, *refs):
    for index, target in enumerate(refs[-targets:]):

        @pl.when((pl.program_id(0) == index) | (targets == 1))
        def _(target=target):
            for mask, source in enumerate(refs[:sources]):
                at = level_ref[0] ^ mask
                place = target.at[0, :, pl.ds(at, 1)] if targets == 1 else target.at[:, pl.ds(at, 1)]
                place[...] = source[...].reshape(place.shape)


def gather_blocks(fourier, received, places, chunk, order_count, apart, after):
    slot, start, width = chunk
    _, blocks, _, rows, _ = fourier.shape
    slots_here = places[2].shape[0] // order_count
    level_count = lax.axis_size("level")
    group = blocks // level_count

    def order_at(step, coordinate):
        return coordinate[0] ^ step if apart else step

    def own_map(step, level, coordinate, slots):
        order = order_at(step, coordinate)
        return (slots[order * slots_here + slot], level[0], 0, 0, start // width)

    def received_map(step, level, coordinate, slots):
        return (order_at(step, coordinate), 0, 0, 0)

    shape = (group, level_count, rows, width)
    if apart:
        out_specs = [pl.BlockSpec(shape, lambda step, *places: (0, 0, 0, 0))] * order_count
        out_shape = [jax.ShapeDtypeStruct(shape, fourier.dtype)] * order_count
    else:
        out_specs = [pl.BlockSpec((1,) + shape, lambda step, *places: (step, 0, 0, 0, 0))]
        out_shape = [jax.ShapeDtypeStruct((order_count,) + shape, fourier.dtype)]
    return pl.pallas_call(
        functools.partial(gather_kernel, level_count, len(out_shape)),
        grid_spec=pltpu.PrefetchScalarGridSpec(
            num_scalar_prefetch=3,
            grid=(order_count,),
            in_specs=[pl.BlockSpec((1, group, 1, rows, width), own_map)]
            + [pl.BlockSpec((1, group, rows, width), received_map) for _ in received]
            + anywhere(after),
            out_specs=out_specs,
        ),
        out_shape=out_shape,
        compiler_params=params(1),
        cost_estimate=cost(),
        name="gather_blocks",
    )(*places, fourier, *received, *after)


def low_kernel(source_first, count, order_ref, *refs):
    rows_refs, (self_ref, pair_ref) = refs[:count], refs[count : count + 2]
    out_ref, state = refs[-3:-1]
    rows_ref = refs[-1] if count > 1 else rows_refs[0]
    level = pl.program_id(0)
    blocks = out_ref.shape[0]
    bits = blocks.bit_length() - 1
    groups, first, second = rows_ref.shape[:3]

    def block_of(height, block):
        if height:
            return [state[block]]
        if source_first:
            at = (block % first, block // first)
        else:
            at = (block // second, block % second)
        return [rows_ref[(group,) + at] for group in range(groups)]

    for height in range(bits):

        @pl.when(level == height)
        def _(height=height):
            if height == 0 and count > 1:
                for mask, source in enumerate(rows_refs):
                    rows_ref[pl.ds(order_ref[0] ^ mask, 1)] = source[...].reshape(
                        (1,) + source.shape
                    )
            target = out_ref if height == bits - 1 else state
            for low in range(blocks):
                high = low ^ (1 << height)
                if high < low:
                    continue
                values = jnp.concatenate(block_of(height, low) + block_of(height, high), axis=0)
                factors = jnp.concatenate(
                    [
                        jnp.concatenate([self_ref[0, 0, low], pair_ref[0, 0, low]], axis=1),
                        jnp.concatenate([pair_ref[0, 0, high], self_ref[0, 0, high]], axis=1),
                    ],
                    axis=0,
                )
                mixed = jnp.dot(factors, values, preferred_element_type=jnp.float32)
                mixed = mixed.astype(target.dtype)
                target[low] = mixed[: mixed.shape[0] // 2]
                target[high] = mixed[mixed.shape[0] // 2 :]


def low_levels(rows, order, coeff_self, coeff_pair, slot, source_first, after):
    width = rows[0].shape[-1]
    blocks, cycle = coeff_self.shape[2:4]
    bits = blocks.bit_length() - 1
    factor = pl.BlockSpec((1, 1, blocks, cycle, cycle), lambda level, *order: (level, slot, 0, 0, 0))
    scratch = [pltpu.VMEM((blocks, cycle, width), rows[0].dtype)]
    scratch.append(
        pltpu.VMEM((len(rows),) + rows[0].shape if len(rows) > 1 else (8, 128), rows[0].dtype)
    )
    return pl.pallas_call(
        functools.partial(low_kernel, source_first, len(rows)),
        grid_spec=pltpu.PrefetchScalarGridSpec(
            num_scalar_prefetch=1,
            grid=(bits,),
            in_specs=[
                pl.BlockSpec(value.shape, lambda level, *order, rank=value.ndim: (0,) * rank)
                for value in rows
            ]
            + [factor, factor]
            + anywhere(after),
            out_specs=pl.BlockSpec((blocks, cycle, width), lambda level, *order: (0, 0, 0)),
            scratch_shapes=scratch,
        ),
        out_shape=jax.ShapeDtypeStruct((blocks, cycle, width), rows[0].dtype),
        compiler_params=params(1),
        cost_estimate=cost(),
        name="low_levels",
    )(order, *rows, coeff_self, coeff_pair, *after)


def high_kernel(own_ref, other_ref, self_ref, pair_ref, *refs):
    target = refs[-1]
    lead = len(target.shape) - 3
    for block in range(own_ref.shape[0]):
        factors = jnp.concatenate([self_ref[0, 0, block], pair_ref[0, 0, block]], axis=1)
        values = jnp.concatenate([own_ref[block], other_ref[block]], axis=0)
        mixed = jnp.dot(factors, values, preferred_element_type=jnp.float32)
        target[(0,) * lead + (block,)] = mixed.astype(target.dtype)


def high_level(own, other, coeff_self, coeff_pair, level, slot, after, final=None):
    blocks, cycle, width = own.shape
    step = min(4, blocks)
    value = pl.BlockSpec((step, cycle, width), lambda at: (at, 0, 0))
    factor = pl.BlockSpec((1, 1, step, cycle, cycle), lambda at: (level, slot, at, 0, 0))
    operands = [own, other, coeff_self, coeff_pair]
    in_specs = [value, value, factor, factor]
    aliases = {}
    if final is None:
        out_spec, out_shape = value, jax.ShapeDtypeStruct(own.shape, own.dtype)
    else:
        result, shape, part = final
        out_spec = pl.BlockSpec((1, step, cycle, width), lambda at: (slot, at, 0, part))
        out_shape = jax.ShapeDtypeStruct(shape, own.dtype)
        if result is not None:
            operands.append(result)
            in_specs += anywhere([result])
            aliases = {4: 0}
    return pl.pallas_call(
        high_kernel,
        grid=(blocks // step,),
        in_specs=in_specs + anywhere(after),
        out_specs=out_spec,
        out_shape=out_shape,
        input_output_aliases=aliases,
        compiler_params=params(1),
        cost_estimate=cost(),
        name="high_level",
    )(*operands, *after)


def local(fourier, order_slot, coeff_self, coeff_pair):
    order_count = lax.axis_size("order")
    level_count = lax.axis_size("level")
    levels, orders_here, blocks_here, cycle_rows, _ = coeff_self.shape
    rows_here, columns = fourier.shape[3:]
    local_bits = blocks_here.bit_length() - 1
    steps = levels - local_bits
    group = blocks_here // level_count
    width = columns // COLUMN_PARTS
    chunks = [
        (slot, part * width, width) for slot in range(orders_here) for part in range(COLUMN_PARTS)
    ]
    modes, order = run_order(len(chunks), steps, rows_here % 16 == 0)

    def place(axis):
        return lax.axis_index(axis).astype(jnp.int32).reshape(1)

    places = (place("level"), place("order"), order_slot)
    level_masks = tuple(range(1, level_count))
    shape = (orders_here, blocks_here, cycle_rows, columns)
    outgoing, rows, state = {}, {}, {}
    result = None
    last = []
    for kind, at in order:
        chunk, mode = chunks[at], modes[at]
        slot, start, _ = chunk
        if kind == TAKE:
            masks = () if mode == DIRECT else level_masks
            outgoing[at] = take_rows(fourier, places, chunk, masks, order_count, last)
            last = [outgoing[at][0]]
            if mode == DIRECT:
                value = outgoing[at][0].reshape(
                    order_count * level_count, group, rows_here, width
                )
                value = lax.all_to_all(
                    value, ("order", "level"), split_axis=0, concat_axis=0, tiled=True
                )
                value = value.reshape(order_count, level_count, group, rows_here, width)
                if rows_here % 16:
                    value = value.transpose(1, 2, 0, 3, 4).reshape(
                        1, level_count, group, cycle_rows, width
                    )
                rows[at] = [value]
        elif kind == GATHER:
            received = [swap(value, "level", mask) for value, mask in zip(outgoing[at], level_masks)]
            gathered = gather_blocks(
                fourier, received, places, chunk, order_count, mode == PAIRS, last
            )
            last = [gathered[0]]
            if mode == PAIRS:
                rows[at] = [gathered[0]] + [
                    swap(value, "order", mask) for mask, value in enumerate(gathered) if mask
                ]
            else:
                rows[at] = [
                    lax.all_to_all(gathered[0], "order", split_axis=0, concat_axis=0, tiled=True)
                ]
        elif kind == LOW:
            state[at] = low_levels(
                rows[at], places[1], coeff_self, coeff_pair, slot, mode == DIRECT, last
            )
            last = [state[at]]
        else:
            other = swap(state[at], "level", 1 << (kind - 1))
            final = None
            if kind == steps:
                final = (result, shape, start // width)
                last = [value for value in last if value is not result]
            state[at] = high_level(
                state[at], other, coeff_self, coeff_pair, local_bits + kind - 1, slot, last, final
            )
            last = [state[at]]
            if kind == steps:
                result = state[at]
    return result


def solution(mesh):
    placed = (
        P("freq", None, "level", "order", None),
        P(),
        P(None, "order", "level", None, None),
        P(None, "order", "level", None, None),
    )
    return jax.shard_map(
        local,
        mesh=mesh,
        in_specs=placed,
        out_specs=P(("freq", "order"), "level", None, None),
        check_vma=False,
    )
```

```python
import functools

import jax
import jax.numpy as jnp
from jax import lax
from jax.experimental import pallas as pl
from jax.experimental.pallas import tpu as pltpu
from jax.sharding import PartitionSpec as P

VMEM = 48 * 1024 * 1024
TAKE, GATHER, LOW = "take", "gather", "low"
DIRECT, MIXED, PAIRS = "direct", "mixed", "pairs"
CHUNKS = ((0, 0, 2), (0, 2, 2), (1, 0, 2), (1, 2, 2))
PIECES = (1, 1, 1, 1,)
MODES = (DIRECT, DIRECT, DIRECT, MIXED)
ORDER = (
    (TAKE, 0), (TAKE, 1), (LOW, 0), (TAKE, 2), (1, 0), (TAKE, 3), (LOW, 1), (1, 1), (LOW, 2),
    (GATHER, 3), (2, 0), (1, 2), (LOW, 3), (2, 1), (1, 3), (2, 2), (2, 3),
)


def plan(slots, steps, pairs):
    if steps == 2 and pairs and slots == 1 + max(slot for slot, _, _ in CHUNKS):
        return CHUNKS, PIECES, MODES, ORDER
    chunks = [(slot, part, 2) for slot in range(slots) for part in (0, 2)]
    count = len(chunks)
    order = []
    for turn in range(count + steps + 2):
        jobs = [(TAKE, turn), (LOW, turn - 1)]
        jobs += [(step, turn - 1 - step) for step in range(1, steps + 1)]
        order += [job for job in jobs if 0 <= job[1] < count]
    return chunks, (1,) * count, (DIRECT,) * count, order


def params(steps):
    return pltpu.CompilerParams(
        dimension_semantics=("arbitrary",) * steps, vmem_limit_bytes=VMEM
    )


def cost():
    return pl.CostEstimate(flops=0, bytes_accessed=1024, transcendentals=0)


def anywhere(values):
    return [pl.BlockSpec(memory_space=pl.ANY)] * len(values)


def swap(value, axis, mask):
    pairs = [(source, source ^ mask) for source in range(lax.axis_size(axis))]
    return lax.ppermute(value, axis, pairs)


def copy_kernel(count, level_ref, order_ref, slot_ref, *refs):
    for source, target in zip(refs[:count], refs[-count:]):
        target[...] = source[...].reshape(target.shape)


def take_rows(fourier, places, chunk, masks, order_count, after):
    slot, start, width = chunk
    _, blocks, _, rows, _ = fourier.shape
    slots_here = places[2].shape[0] // order_count
    group = blocks // lax.axis_size("level") if masks else blocks

    def source_map(mask, order, level, coordinate, slots):
        part = level[0] ^ mask if masks else 0
        return (slots[order * slots_here + slot], part, 0, 0, start // width)

    shape = (order_count, group, rows, width)
    return pl.pallas_call(
        functools.partial(copy_kernel, len(masks) or 1),
        grid_spec=pltpu.PrefetchScalarGridSpec(
            num_scalar_prefetch=3,
            grid=(order_count,),
            in_specs=[
                pl.BlockSpec((1, group, 1, rows, width), functools.partial(source_map, mask))
                for mask in masks or (0,)
            ]
            + anywhere(after),
            out_specs=[
                pl.BlockSpec((1,) + shape[1:], lambda order, *places: (order, 0, 0, 0))
                for _ in masks or (0,)
            ],
        ),
        out_shape=[jax.ShapeDtypeStruct(shape, fourier.dtype) for _ in masks or (0,)],
        compiler_params=params(1),
        cost_estimate=cost(),
        name="take_rows",
    )(*places, *[fourier] * (len(masks) or 1), *after)


def gather_kernel(sources, targets, level_ref, order_ref, slot_ref, *refs):
    for index, target in enumerate(refs[-targets:]):

        @pl.when((pl.program_id(0) == index) | (targets == 1))
        def _(target=target):
            for mask, source in enumerate(refs[:sources]):
                at = level_ref[0] ^ mask
                place = target.at[0, :, pl.ds(at, 1)] if targets == 1 else target.at[:, pl.ds(at, 1)]
                place[...] = source[...].reshape(place.shape)


def gather_blocks(fourier, received, places, chunk, order_count, apart, after):
    slot, start, width = chunk
    _, blocks, _, rows, _ = fourier.shape
    slots_here = places[2].shape[0] // order_count
    level_count = lax.axis_size("level")
    group = blocks // level_count

    def order_at(step, coordinate):
        return coordinate[0] ^ step if apart else step

    def own_map(step, level, coordinate, slots):
        order = order_at(step, coordinate)
        return (slots[order * slots_here + slot], level[0], 0, 0, start // width)

    def received_map(step, level, coordinate, slots):
        return (order_at(step, coordinate), 0, 0, 0)

    shape = (group, level_count, rows, width)
    if apart:
        out_specs = [pl.BlockSpec(shape, lambda step, *places: (0, 0, 0, 0))] * order_count
        out_shape = [jax.ShapeDtypeStruct(shape, fourier.dtype)] * order_count
    else:
        out_specs = [pl.BlockSpec((1,) + shape, lambda step, *places: (step, 0, 0, 0, 0))]
        out_shape = [jax.ShapeDtypeStruct((order_count,) + shape, fourier.dtype)]
    return pl.pallas_call(
        functools.partial(gather_kernel, level_count, len(out_shape)),
        grid_spec=pltpu.PrefetchScalarGridSpec(
            num_scalar_prefetch=3,
            grid=(order_count,),
            in_specs=[pl.BlockSpec((1, group, 1, rows, width), own_map)]
            + [pl.BlockSpec((1, group, rows, width), received_map) for _ in received]
            + anywhere(after),
            out_specs=out_specs,
        ),
        out_shape=out_shape,
        compiler_params=params(1),
        cost_estimate=cost(),
        name="gather_blocks",
    )(*places, fourier, *received, *after)


def low_kernel(source_first, count, pieces, order_ref, *refs):
    rows_refs, (self_ref, pair_ref) = refs[:count], refs[count : count + 2]
    out_refs, state = refs[-2 - pieces : -2], refs[-2]
    rows_ref = refs[-1] if count > 1 else rows_refs[0]
    level = pl.program_id(0)
    blocks = state.shape[0]
    bits = blocks.bit_length() - 1
    groups, first, second = rows_ref.shape[:3]

    def block_of(height, block):
        if height:
            return [state[block]]
        if source_first:
            at = (block % first, block // first)
        else:
            at = (block // second, block % second)
        return [rows_ref[(group,) + at] for group in range(groups)]

    for height in range(bits):

        @pl.when(level == height)
        def _(height=height):
            if height == 0 and count > 1:
                for mask, source in enumerate(rows_refs):
                    rows_ref[pl.ds(order_ref[0] ^ mask, 1)] = source[...].reshape(
                        (1,) + source.shape
                    )
            targets = out_refs if height == bits - 1 else (state,)
            for low in range(blocks):
                high = low ^ (1 << height)
                if high < low:
                    continue
                values = jnp.concatenate(block_of(height, low) + block_of(height, high), axis=0)
                factors = jnp.concatenate(
                    [
                        jnp.concatenate([self_ref[0, 0, low], pair_ref[0, 0, low]], axis=1),
                        jnp.concatenate([pair_ref[0, 0, high], self_ref[0, 0, high]], axis=1),
                    ],
                    axis=0,
                )
                mixed = jnp.dot(factors, values, preferred_element_type=jnp.float32)
                mixed = mixed.astype(state.dtype)
                half, width = mixed.shape[0] // 2, mixed.shape[1] // len(targets)
                for piece, target in enumerate(targets):
                    columns = slice(piece * width, (piece + 1) * width)
                    target[low] = mixed[:half, columns]
                    target[high] = mixed[half:, columns]


def low_levels(rows, order, coeff_self, coeff_pair, slot, source_first, pieces, after):
    rows = [pltpu.with_memory_space_constraint(value, pltpu.HBM) for value in rows]
    width = rows[0].shape[-1]
    blocks, cycle = coeff_self.shape[2:4]
    bits = blocks.bit_length() - 1
    shape = (blocks, cycle, width // pieces)
    factor = pl.BlockSpec((1, 1, blocks, cycle, cycle), lambda level, *order: (level, slot, 0, 0, 0))
    scratch = [pltpu.VMEM((blocks, cycle, width), rows[0].dtype)]
    scratch.append(
        pltpu.VMEM((len(rows),) + rows[0].shape if len(rows) > 1 else (8, 128), rows[0].dtype)
    )
    return pl.pallas_call(
        functools.partial(low_kernel, source_first, len(rows), pieces),
        grid_spec=pltpu.PrefetchScalarGridSpec(
            num_scalar_prefetch=1,
            grid=(bits,),
            in_specs=[
                pl.BlockSpec(value.shape, lambda level, *order, rank=value.ndim: (0,) * rank)
                for value in rows
            ]
            + [factor, factor]
            + anywhere(after),
            out_specs=[pl.BlockSpec(shape, lambda level, *order: (0, 0, 0))] * pieces,
            scratch_shapes=scratch,
        ),
        out_shape=[jax.ShapeDtypeStruct(shape, rows[0].dtype)] * pieces,
        compiler_params=params(1),
        cost_estimate=cost(),
        name="low_levels",
    )(order, *rows, coeff_self, coeff_pair, *after)


def high_kernel(own_ref, other_ref, self_ref, pair_ref, *refs):
    target = refs[-1]
    lead = len(target.shape) - 3
    for block in range(own_ref.shape[0]):
        factors = jnp.concatenate([self_ref[0, 0, block], pair_ref[0, 0, block]], axis=1)
        values = jnp.concatenate([own_ref[block], other_ref[block]], axis=0)
        mixed = jnp.dot(factors, values, preferred_element_type=jnp.float32)
        target[(0,) * lead + (block,)] = mixed.astype(target.dtype)


def high_level(own, other, coeff_self, coeff_pair, level, slot, after, final=None):
    blocks, cycle, width = own.shape
    step = min(4, blocks)
    value = pl.BlockSpec((step, cycle, width), lambda at: (at, 0, 0))
    factor = pl.BlockSpec((1, 1, step, cycle, cycle), lambda at: (level, slot, at, 0, 0))
    operands = [own, other, coeff_self, coeff_pair]
    in_specs = [value, value, factor, factor]
    aliases = {}
    if final is None:
        out_spec, out_shape = value, jax.ShapeDtypeStruct(own.shape, own.dtype)
    else:
        result, shape, part = final
        out_spec = pl.BlockSpec((1, step, cycle, width), lambda at: (slot, at, 0, part))
        out_shape = jax.ShapeDtypeStruct(shape, own.dtype)
        if result is not None:
            operands.append(result)
            in_specs += anywhere([result])
            aliases = {4: 0}
    return pl.pallas_call(
        high_kernel,
        grid=(blocks // step,),
        in_specs=in_specs + anywhere(after),
        out_specs=out_spec,
        out_shape=out_shape,
        input_output_aliases=aliases,
        compiler_params=params(1),
        cost_estimate=cost(),
        name="high_level",
    )(*operands, *after)


def local(fourier, order_slot, coeff_self, coeff_pair):
    fourier = pltpu.with_memory_space_constraint(fourier, pltpu.HBM)
    order_count = lax.axis_size("order")
    level_count = lax.axis_size("level")
    levels, orders_here, blocks_here, cycle_rows, _ = coeff_self.shape
    rows_here, columns = fourier.shape[3:]
    local_bits = blocks_here.bit_length() - 1
    steps = levels - local_bits
    group = blocks_here // level_count
    parts, pieces, modes, order = plan(orders_here, steps, rows_here % 16 == 0)
    quarter = columns // 4
    chunks = [(slot, first * quarter, count * quarter) for slot, first, count in parts]

    def place(axis):
        return lax.axis_index(axis).astype(jnp.int32).reshape(1)

    places = (place("level"), place("order"), order_slot)
    level_masks = tuple(range(1, level_count))
    shape = (orders_here, blocks_here, cycle_rows, columns)
    where = [
        (at, slot, start + piece * (width // count), width // count)
        for at, ((slot, start, width), count) in enumerate(zip(chunks, pieces))
        for piece in range(count)
    ]
    outgoing, rows, state = {}, {}, {}
    result = None
    last = []
    for kind, at in order:
        if kind in (TAKE, GATHER, LOW):
            chunk, mode = chunks[at], modes[at]
            slot, start, width = chunk
        if kind == TAKE:
            masks = () if mode == DIRECT else level_masks
            outgoing[at] = take_rows(fourier, places, chunk, masks, order_count, last)
            last = [outgoing[at][0]]
            if mode == DIRECT:
                value = outgoing[at][0].reshape(
                    order_count * level_count, group, rows_here, width
                )
                value = lax.all_to_all(
                    value, ("order", "level"), split_axis=0, concat_axis=0, tiled=True
                )
                value = value.reshape(order_count, level_count, group, rows_here, width)
                if rows_here % 16:
                    value = value.transpose(1, 2, 0, 3, 4).reshape(
                        1, level_count, group, cycle_rows, width
                    )
                rows[at] = [value]
        elif kind == GATHER:
            received = [swap(value, "level", mask) for value, mask in zip(outgoing[at], level_masks)]
            gathered = gather_blocks(
                fourier, received, places, chunk, order_count, mode == PAIRS, last
            )
            last = [gathered[0]]
            if mode == PAIRS:
                rows[at] = [gathered[0]] + [
                    swap(value, "order", mask) for mask, value in enumerate(gathered) if mask
                ]
            else:
                rows[at] = [
                    lax.all_to_all(gathered[0], "order", split_axis=0, concat_axis=0, tiled=True)
                ]
        elif kind == LOW:
            lowest = low_levels(
                rows[at],
                places[1],
                coeff_self,
                coeff_pair,
                slot,
                mode == DIRECT,
                pieces[at],
                last,
            )
            last = [lowest[0]]
            first = [piece for piece, (chunk, *_) in enumerate(where) if chunk == at][0]
            state.update(enumerate(lowest, first))
        else:
            _, slot, start, width = where[at]
            other = swap(state[at], "level", 1 << (kind - 1))
            final = None
            if kind == steps:
                final = (result, shape, start // width)
                last = [value for value in last if value is not result]
            state[at] = high_level(
                state[at], other, coeff_self, coeff_pair, local_bits + kind - 1, slot, last, final
            )
            last = [state[at]]
            if kind == steps:
                result = state[at]
    return result


def solution(mesh):
    placed = (
        P("freq", None, "level", "order", None),
        P(),
        P(None, "order", "level", None, None),
        P(None, "order", "level", None, None),
    )
    return jax.shard_map(
        local,
        mesh=mesh,
        in_specs=placed,
        out_specs=P(("freq", "order"), "level", None, None),
        check_vma=False,
    )
```

```python
import functools

import jax
import jax.numpy as jnp
from jax import lax
from jax.experimental import pallas as pl
from jax.experimental.pallas import tpu as pltpu
from jax.sharding import PartitionSpec as P

VMEM = 48 * 1024 * 1024
TAKE, GATHER, LOW = "take", "gather", "low"
DIRECT, MIXED, PAIRS = "direct", "mixed", "pairs"
CHUNKS = ((0, 0, 2), (0, 2, 2), (1, 0, 2), (1, 2, 2))
PIECES = (1, 1, 1, 1,)
MODES = (DIRECT, DIRECT, DIRECT, MIXED)
ORDER = (
    (TAKE, 0), (TAKE, 1), (LOW, 0), (TAKE, 2), (1, 0), (TAKE, 3), (LOW, 1), (1, 1), (LOW, 2),
    (GATHER, 3), (2, 0), (1, 2), (LOW, 3), (2, 1), (1, 3), (2, 2), (2, 3),
)


def plan(slots, steps, pairs):
    if steps == 2 and pairs and slots == 1 + max(slot for slot, _, _ in CHUNKS):
        return CHUNKS, PIECES, MODES, ORDER
    chunks = [(slot, part, 2) for slot in range(slots) for part in (0, 2)]
    count = len(chunks)
    order = []
    for turn in range(count + steps + 2):
        jobs = [(TAKE, turn), (LOW, turn - 1)]
        jobs += [(step, turn - 1 - step) for step in range(1, steps + 1)]
        order += [job for job in jobs if 0 <= job[1] < count]
    return chunks, (1,) * count, (DIRECT,) * count, order


def params(steps):
    return pltpu.CompilerParams(
        dimension_semantics=("arbitrary",) * steps, vmem_limit_bytes=VMEM
    )


def cost():
    return pl.CostEstimate(flops=0, bytes_accessed=1024, transcendentals=0)


def anywhere(values):
    return [pl.BlockSpec(memory_space=pl.ANY)] * len(values)


def swap(value, axis, mask):
    pairs = [(source, source ^ mask) for source in range(lax.axis_size(axis))]
    return lax.ppermute(value, axis, pairs)


def copy_kernel(count, level_ref, order_ref, slot_ref, *refs):
    for source, target in zip(refs[:count], refs[-count:]):
        target[...] = source[...].reshape(target.shape)


def take_rows(fourier, places, chunk, masks, order_count, after):
    slot, start, width = chunk
    _, blocks, _, rows, _ = fourier.shape
    slots_here = places[2].shape[0] // order_count
    group = blocks // lax.axis_size("level") if masks else blocks

    def source_map(mask, order, level, coordinate, slots):
        part = level[0] ^ mask if masks else 0
        return (slots[order * slots_here + slot], part, 0, 0, start // width)

    shape = (order_count, group, rows, width)
    return pl.pallas_call(
        functools.partial(copy_kernel, len(masks) or 1),
        grid_spec=pltpu.PrefetchScalarGridSpec(
            num_scalar_prefetch=3,
            grid=(order_count,),
            in_specs=[
                pl.BlockSpec((1, group, 1, rows, width), functools.partial(source_map, mask))
                for mask in masks or (0,)
            ]
            + anywhere(after),
            out_specs=[
                pl.BlockSpec((1,) + shape[1:], lambda order, *places: (order, 0, 0, 0))
                for _ in masks or (0,)
            ],
        ),
        out_shape=[jax.ShapeDtypeStruct(shape, fourier.dtype) for _ in masks or (0,)],
        compiler_params=params(1),
        cost_estimate=cost(),
        name="take_rows",
    )(*places, *[fourier] * (len(masks) or 1), *after)


def gather_kernel(sources, targets, level_ref, order_ref, slot_ref, *refs):
    for index, target in enumerate(refs[-targets:]):

        @pl.when((pl.program_id(0) == index) | (targets == 1))
        def _(target=target):
            for mask, source in enumerate(refs[:sources]):
                at = level_ref[0] ^ mask
                place = target.at[0, :, pl.ds(at, 1)] if targets == 1 else target.at[:, pl.ds(at, 1)]
                place[...] = source[...].reshape(place.shape)


def gather_blocks(fourier, received, places, chunk, order_count, apart, after):
    slot, start, width = chunk
    _, blocks, _, rows, _ = fourier.shape
    slots_here = places[2].shape[0] // order_count
    level_count = lax.axis_size("level")
    group = blocks // level_count

    def order_at(step, coordinate):
        return coordinate[0] ^ step if apart else step

    def own_map(step, level, coordinate, slots):
        order = order_at(step, coordinate)
        return (slots[order * slots_here + slot], level[0], 0, 0, start // width)

    def received_map(step, level, coordinate, slots):
        return (order_at(step, coordinate), 0, 0, 0)

    shape = (group, level_count, rows, width)
    if apart:
        out_specs = [pl.BlockSpec(shape, lambda step, *places: (0, 0, 0, 0))] * order_count
        out_shape = [jax.ShapeDtypeStruct(shape, fourier.dtype)] * order_count
    else:
        out_specs = [pl.BlockSpec((1,) + shape, lambda step, *places: (step, 0, 0, 0, 0))]
        out_shape = [jax.ShapeDtypeStruct((order_count,) + shape, fourier.dtype)]
    return pl.pallas_call(
        functools.partial(gather_kernel, level_count, len(out_shape)),
        grid_spec=pltpu.PrefetchScalarGridSpec(
            num_scalar_prefetch=3,
            grid=(order_count,),
            in_specs=[pl.BlockSpec((1, group, 1, rows, width), own_map)]
            + [pl.BlockSpec((1, group, rows, width), received_map) for _ in received]
            + anywhere(after),
            out_specs=out_specs,
        ),
        out_shape=out_shape,
        compiler_params=params(1),
        cost_estimate=cost(),
        name="gather_blocks",
    )(*places, fourier, *received, *after)


def low_kernel(source_first, count, pieces, order_ref, *refs):
    rows_refs, (self_ref, pair_ref) = refs[:count], refs[count : count + 2]
    out_refs, state = refs[-2 - pieces : -2], refs[-2]
    rows_ref = refs[-1] if count > 1 else rows_refs[0]
    level = pl.program_id(0)
    blocks = state.shape[0]
    bits = blocks.bit_length() - 1
    groups, first, second = rows_ref.shape[:3]

    def block_of(height, block):
        if height:
            return [state[block]]
        if source_first:
            at = (block % first, block // first)
        else:
            at = (block // second, block % second)
        return [rows_ref[(group,) + at] for group in range(groups)]

    for height in range(bits):

        @pl.when(level == height)
        def _(height=height):
            if height == 0 and count > 1:
                for mask, source in enumerate(rows_refs):
                    rows_ref[pl.ds(order_ref[0] ^ mask, 1)] = source[...].reshape(
                        (1,) + source.shape
                    )
            targets = out_refs if height == bits - 1 else (state,)
            for low in range(blocks):
                high = low ^ (1 << height)
                if high < low:
                    continue
                values = jnp.concatenate(block_of(height, low) + block_of(height, high), axis=0)
                factors = jnp.concatenate(
                    [
                        jnp.concatenate([self_ref[0, 0, low], pair_ref[0, 0, low]], axis=1),
                        jnp.concatenate([pair_ref[0, 0, high], self_ref[0, 0, high]], axis=1),
                    ],
                    axis=0,
                )
                mixed = jnp.dot(factors, values, preferred_element_type=jnp.float32)
                mixed = mixed.astype(state.dtype)
                half, width = mixed.shape[0] // 2, mixed.shape[1] // len(targets)
                for piece, target in enumerate(targets):
                    columns = slice(piece * width, (piece + 1) * width)
                    target[low] = mixed[:half, columns]
                    target[high] = mixed[half:, columns]


def low_levels(rows, order, coeff_self, coeff_pair, slot, source_first, pieces, after):
    rows = [pltpu.with_memory_space_constraint(value, pltpu.HBM) for value in rows]
    width = rows[0].shape[-1]
    blocks, cycle = coeff_self.shape[2:4]
    bits = blocks.bit_length() - 1
    shape = (blocks, cycle, width // pieces)
    factor = pl.BlockSpec((1, 1, blocks, cycle, cycle), lambda level, *order: (level, slot, 0, 0, 0))
    scratch = [pltpu.VMEM((blocks, cycle, width), rows[0].dtype)]
    scratch.append(
        pltpu.VMEM((len(rows),) + rows[0].shape if len(rows) > 1 else (8, 128), rows[0].dtype)
    )
    return pl.pallas_call(
        functools.partial(low_kernel, source_first, len(rows), pieces),
        grid_spec=pltpu.PrefetchScalarGridSpec(
            num_scalar_prefetch=1,
            grid=(bits,),
            in_specs=[
                pl.BlockSpec(value.shape, lambda level, *order, rank=value.ndim: (0,) * rank)
                for value in rows
            ]
            + [factor, factor]
            + anywhere(after),
            out_specs=[pl.BlockSpec(shape, lambda level, *order: (0, 0, 0))] * pieces,
            scratch_shapes=scratch,
        ),
        out_shape=[jax.ShapeDtypeStruct(shape, rows[0].dtype)] * pieces,
        compiler_params=params(1),
        cost_estimate=cost(),
        name="low_levels",
    )(order, *rows, coeff_self, coeff_pair, *after)


def high_kernel(own_ref, other_ref, self_ref, pair_ref, *refs):
    target = refs[-1]
    lead = len(target.shape) - 3
    for block in range(own_ref.shape[0]):
        factors = jnp.concatenate([self_ref[0, 0, block], pair_ref[0, 0, block]], axis=1)
        values = jnp.concatenate([own_ref[block], other_ref[block]], axis=0)
        mixed = jnp.dot(factors, values, preferred_element_type=jnp.float32)
        target[(0,) * lead + (block,)] = mixed.astype(target.dtype)


def high_level(own, other, coeff_self, coeff_pair, level, slot, after, final=None):
    blocks, cycle, width = own.shape
    step = min(8, blocks)
    value = pl.BlockSpec((step, cycle, width), lambda at: (at, 0, 0))
    factor = pl.BlockSpec((1, 1, step, cycle, cycle), lambda at: (level, slot, at, 0, 0))
    operands = [own, other, coeff_self, coeff_pair]
    in_specs = [value, value, factor, factor]
    aliases = {}
    if final is None:
        out_spec, out_shape = value, jax.ShapeDtypeStruct(own.shape, own.dtype)
    else:
        result, shape, part = final
        out_spec = pl.BlockSpec((1, step, cycle, width), lambda at: (slot, at, 0, part))
        out_shape = jax.ShapeDtypeStruct(shape, own.dtype)
        if result is not None:
            operands.append(result)
            in_specs += anywhere([result])
            aliases = {4: 0}
    return pl.pallas_call(
        high_kernel,
        grid=(blocks // step,),
        in_specs=in_specs + anywhere(after),
        out_specs=out_spec,
        out_shape=out_shape,
        input_output_aliases=aliases,
        compiler_params=params(1),
        cost_estimate=cost(),
        name="high_level",
    )(*operands, *after)


def local(fourier, order_slot, coeff_self, coeff_pair):
    fourier = pltpu.with_memory_space_constraint(fourier, pltpu.HBM)
    order_count = lax.axis_size("order")
    level_count = lax.axis_size("level")
    levels, orders_here, blocks_here, cycle_rows, _ = coeff_self.shape
    rows_here, columns = fourier.shape[3:]
    local_bits = blocks_here.bit_length() - 1
    steps = levels - local_bits
    group = blocks_here // level_count
    parts, pieces, modes, order = plan(orders_here, steps, rows_here % 16 == 0)
    quarter = columns // 4
    chunks = [(slot, first * quarter, count * quarter) for slot, first, count in parts]

    def place(axis):
        return lax.axis_index(axis).astype(jnp.int32).reshape(1)

    places = (place("level"), place("order"), order_slot)
    level_masks = tuple(range(1, level_count))
    shape = (orders_here, blocks_here, cycle_rows, columns)
    where = [
        (at, slot, start + piece * (width // count), width // count)
        for at, ((slot, start, width), count) in enumerate(zip(chunks, pieces))
        for piece in range(count)
    ]
    outgoing, rows, state = {}, {}, {}
    result = None
    last = []
    for kind, at in order:
        if kind in (TAKE, GATHER, LOW):
            chunk, mode = chunks[at], modes[at]
            slot, start, width = chunk
        if kind == TAKE:
            masks = () if mode == DIRECT else level_masks
            outgoing[at] = take_rows(fourier, places, chunk, masks, order_count, last)
            last = [outgoing[at][0]]
            if mode == DIRECT:
                value = outgoing[at][0].reshape(
                    order_count * level_count, group, rows_here, width
                )
                value = lax.all_to_all(
                    value, ("order", "level"), split_axis=0, concat_axis=0, tiled=True
                )
                value = value.reshape(order_count, level_count, group, rows_here, width)
                if rows_here % 16:
                    value = value.transpose(1, 2, 0, 3, 4).reshape(
                        1, level_count, group, cycle_rows, width
                    )
                rows[at] = [value]
        elif kind == GATHER:
            received = [swap(value, "level", mask) for value, mask in zip(outgoing[at], level_masks)]
            gathered = gather_blocks(
                fourier, received, places, chunk, order_count, mode == PAIRS, last
            )
            last = [gathered[0]]
            if mode == PAIRS:
                rows[at] = [gathered[0]] + [
                    swap(value, "order", mask) for mask, value in enumerate(gathered) if mask
                ]
            else:
                rows[at] = [
                    lax.all_to_all(gathered[0], "order", split_axis=0, concat_axis=0, tiled=True)
                ]
        elif kind == LOW:
            lowest = low_levels(
                rows[at],
                places[1],
                coeff_self,
                coeff_pair,
                slot,
                mode == DIRECT,
                pieces[at],
                last,
            )
            last = [lowest[0]]
            first = [piece for piece, (chunk, *_) in enumerate(where) if chunk == at][0]
            state.update(enumerate(lowest, first))
        else:
            _, slot, start, width = where[at]
            other = swap(state[at], "level", 1 << (kind - 1))
            final = None
            if kind == steps:
                final = (result, shape, start // width)
                last = [value for value in last if value is not result]
            state[at] = high_level(
                state[at], other, coeff_self, coeff_pair, local_bits + kind - 1, slot, last, final
            )
            last = [state[at]]
            if kind == steps:
                result = state[at]
    return result


def solution(mesh):
    placed = (
        P("freq", None, "level", "order", None),
        P(),
        P(None, "order", "level", None, None),
        P(None, "order", "level", None, None),
    )
    return jax.shard_map(
        local,
        mesh=mesh,
        in_specs=placed,
        out_specs=P(("freq", "order"), "level", None, None),
        check_vma=False,
    )
```

```python
import functools

import jax
import jax.numpy as jnp
from jax import lax
from jax.experimental import pallas as pl
from jax.experimental.pallas import tpu as pltpu
from jax.sharding import PartitionSpec as P

VMEM = 48 * 1024 * 1024
TAKE, GATHER, LOW = "take", "gather", "low"
DIRECT, MIXED, PAIRS = "direct", "mixed", "pairs"
CHUNKS = ((0, 0, 2), (0, 2, 2), (1, 0, 2), (1, 2, 2))
PIECES = (1, 1, 1, 1,)
MODES = (DIRECT, DIRECT, DIRECT, MIXED)
ORDER = (
    (TAKE, 0), (TAKE, 1), (LOW, 0), (TAKE, 3), (TAKE, 2), (1, 0), (LOW, 1), (1, 1), (LOW, 2),
    (GATHER, 3), (2, 0), (1, 2), (LOW, 3), (2, 1), (1, 3), (2, 2), (2, 3),
)


def plan(slots, steps, pairs):
    if steps == 2 and pairs and slots == 1 + max(slot for slot, _, _ in CHUNKS):
        return CHUNKS, PIECES, MODES, ORDER
    chunks = [(slot, part, 2) for slot in range(slots) for part in (0, 2)]
    count = len(chunks)
    order = []
    for turn in range(count + steps + 2):
        jobs = [(TAKE, turn), (LOW, turn - 1)]
        jobs += [(step, turn - 1 - step) for step in range(1, steps + 1)]
        order += [job for job in jobs if 0 <= job[1] < count]
    return chunks, (1,) * count, (DIRECT,) * count, order


def params(steps):
    return pltpu.CompilerParams(
        dimension_semantics=("arbitrary",) * steps, vmem_limit_bytes=VMEM
    )


def cost():
    return pl.CostEstimate(flops=0, bytes_accessed=1024, transcendentals=0)


def anywhere(values):
    return [pl.BlockSpec(memory_space=pl.ANY)] * len(values)


def swap(value, axis, mask):
    pairs = [(source, source ^ mask) for source in range(lax.axis_size(axis))]
    return lax.ppermute(value, axis, pairs)


def copy_kernel(count, level_ref, order_ref, slot_ref, *refs):
    for source, target in zip(refs[:count], refs[-count:]):
        target[...] = source[...].reshape(target.shape)


def take_rows(fourier, places, chunk, masks, order_count, after):
    slot, start, width = chunk
    _, blocks, _, rows, _ = fourier.shape
    slots_here = places[2].shape[0] // order_count
    group = blocks // lax.axis_size("level") if masks else blocks

    def source_map(mask, order, level, coordinate, slots):
        part = level[0] ^ mask if masks else 0
        return (slots[order * slots_here + slot], part, 0, 0, start // width)

    shape = (order_count, group, rows, width)
    return pl.pallas_call(
        functools.partial(copy_kernel, len(masks) or 1),
        grid_spec=pltpu.PrefetchScalarGridSpec(
            num_scalar_prefetch=3,
            grid=(order_count,),
            in_specs=[
                pl.BlockSpec((1, group, 1, rows, width), functools.partial(source_map, mask))
                for mask in masks or (0,)
            ]
            + anywhere(after),
            out_specs=[
                pl.BlockSpec((1,) + shape[1:], lambda order, *places: (order, 0, 0, 0))
                for _ in masks or (0,)
            ],
        ),
        out_shape=[jax.ShapeDtypeStruct(shape, fourier.dtype) for _ in masks or (0,)],
        compiler_params=params(1),
        cost_estimate=cost(),
        name="take_rows",
    )(*places, *[fourier] * (len(masks) or 1), *after)


def gather_kernel(sources, targets, level_ref, order_ref, slot_ref, *refs):
    for index, target in enumerate(refs[-targets:]):

        @pl.when((pl.program_id(0) == index) | (targets == 1))
        def _(target=target):
            for mask, source in enumerate(refs[:sources]):
                at = level_ref[0] ^ mask
                place = target.at[0, :, pl.ds(at, 1)] if targets == 1 else target.at[:, pl.ds(at, 1)]
                place[...] = source[...].reshape(place.shape)


def gather_blocks(fourier, received, places, chunk, order_count, apart, after):
    slot, start, width = chunk
    _, blocks, _, rows, _ = fourier.shape
    slots_here = places[2].shape[0] // order_count
    level_count = lax.axis_size("level")
    group = blocks // level_count

    def order_at(step, coordinate):
        return coordinate[0] ^ step if apart else step

    def own_map(step, level, coordinate, slots):
        order = order_at(step, coordinate)
        return (slots[order * slots_here + slot], level[0], 0, 0, start // width)

    def received_map(step, level, coordinate, slots):
        return (order_at(step, coordinate), 0, 0, 0)

    shape = (group, level_count, rows, width)
    if apart:
        out_specs = [pl.BlockSpec(shape, lambda step, *places: (0, 0, 0, 0))] * order_count
        out_shape = [jax.ShapeDtypeStruct(shape, fourier.dtype)] * order_count
    else:
        out_specs = [pl.BlockSpec((1,) + shape, lambda step, *places: (step, 0, 0, 0, 0))]
        out_shape = [jax.ShapeDtypeStruct((order_count,) + shape, fourier.dtype)]
    return pl.pallas_call(
        functools.partial(gather_kernel, level_count, len(out_shape)),
        grid_spec=pltpu.PrefetchScalarGridSpec(
            num_scalar_prefetch=3,
            grid=(order_count,),
            in_specs=[pl.BlockSpec((1, group, 1, rows, width), own_map)]
            + [pl.BlockSpec((1, group, rows, width), received_map) for _ in received]
            + anywhere(after),
            out_specs=out_specs,
        ),
        out_shape=out_shape,
        compiler_params=params(1),
        cost_estimate=cost(),
        name="gather_blocks",
    )(*places, fourier, *received, *after)


def low_kernel(source_first, count, pieces, order_ref, *refs):
    rows_refs, (self_ref, pair_ref) = refs[:count], refs[count : count + 2]
    out_refs, state = refs[-2 - pieces : -2], refs[-2]
    rows_ref = refs[-1] if count > 1 else rows_refs[0]
    level = pl.program_id(0)
    blocks = state.shape[0]
    bits = blocks.bit_length() - 1
    groups, first, second = rows_ref.shape[:3]

    def block_of(height, block):
        if height:
            return [state[block]]
        if source_first:
            at = (block % first, block // first)
        else:
            at = (block // second, block % second)
        return [rows_ref[(group,) + at] for group in range(groups)]

    for height in range(bits):

        @pl.when(level == height)
        def _(height=height):
            if height == 0 and count > 1:
                for mask, source in enumerate(rows_refs):
                    rows_ref[pl.ds(order_ref[0] ^ mask, 1)] = source[...].reshape(
                        (1,) + source.shape
                    )
            targets = out_refs if height == bits - 1 else (state,)
            for low in range(blocks):
                high = low ^ (1 << height)
                if high < low:
                    continue
                values = jnp.concatenate(block_of(height, low) + block_of(height, high), axis=0)
                factors = jnp.concatenate(
                    [
                        jnp.concatenate([self_ref[0, 0, low], pair_ref[0, 0, low]], axis=1),
                        jnp.concatenate([pair_ref[0, 0, high], self_ref[0, 0, high]], axis=1),
                    ],
                    axis=0,
                )
                mixed = jnp.dot(factors, values, preferred_element_type=jnp.float32)
                mixed = mixed.astype(state.dtype)
                half, width = mixed.shape[0] // 2, mixed.shape[1] // len(targets)
                for piece, target in enumerate(targets):
                    columns = slice(piece * width, (piece + 1) * width)
                    target[low] = mixed[:half, columns]
                    target[high] = mixed[half:, columns]


def low_levels(rows, order, coeff_self, coeff_pair, slot, source_first, pieces, after):
    rows = [pltpu.with_memory_space_constraint(value, pltpu.HBM) for value in rows]
    width = rows[0].shape[-1]
    blocks, cycle = coeff_self.shape[2:4]
    bits = blocks.bit_length() - 1
    shape = (blocks, cycle, width // pieces)
    factor = pl.BlockSpec((1, 1, blocks, cycle, cycle), lambda level, *order: (level, slot, 0, 0, 0))
    scratch = [pltpu.VMEM((blocks, cycle, width), rows[0].dtype)]
    scratch.append(
        pltpu.VMEM((len(rows),) + rows[0].shape if len(rows) > 1 else (8, 128), rows[0].dtype)
    )
    return pl.pallas_call(
        functools.partial(low_kernel, source_first, len(rows), pieces),
        grid_spec=pltpu.PrefetchScalarGridSpec(
            num_scalar_prefetch=1,
            grid=(bits,),
            in_specs=[
                pl.BlockSpec(value.shape, lambda level, *order, rank=value.ndim: (0,) * rank)
                for value in rows
            ]
            + [factor, factor]
            + anywhere(after),
            out_specs=[pl.BlockSpec(shape, lambda level, *order: (0, 0, 0))] * pieces,
            scratch_shapes=scratch,
        ),
        out_shape=[jax.ShapeDtypeStruct(shape, rows[0].dtype)] * pieces,
        compiler_params=params(1),
        cost_estimate=cost(),
        name="low_levels",
    )(order, *rows, coeff_self, coeff_pair, *after)


def high_kernel(own_ref, other_ref, self_ref, pair_ref, *refs):
    target = refs[-1]
    lead = len(target.shape) - 3
    for block in range(own_ref.shape[0]):
        factors = jnp.concatenate([self_ref[0, 0, block], pair_ref[0, 0, block]], axis=1)
        values = jnp.concatenate([own_ref[block], other_ref[block]], axis=0)
        mixed = jnp.dot(factors, values, preferred_element_type=jnp.float32)
        target[(0,) * lead + (block,)] = mixed.astype(target.dtype)


def high_level(own, other, coeff_self, coeff_pair, level, slot, after, final=None):
    blocks, cycle, width = own.shape
    step = min(8, blocks)
    value = pl.BlockSpec((step, cycle, width), lambda at: (at, 0, 0))
    factor = pl.BlockSpec((1, 1, step, cycle, cycle), lambda at: (level, slot, at, 0, 0))
    operands = [own, other, coeff_self, coeff_pair]
    in_specs = [value, value, factor, factor]
    aliases = {}
    if final is None:
        out_spec, out_shape = value, jax.ShapeDtypeStruct(own.shape, own.dtype)
    else:
        result, shape, part = final
        out_spec = pl.BlockSpec((1, step, cycle, width), lambda at: (slot, at, 0, part))
        out_shape = jax.ShapeDtypeStruct(shape, own.dtype)
        if result is not None:
            operands.append(result)
            in_specs += anywhere([result])
            aliases = {4: 0}
    return pl.pallas_call(
        high_kernel,
        grid=(blocks // step,),
        in_specs=in_specs + anywhere(after),
        out_specs=out_spec,
        out_shape=out_shape,
        input_output_aliases=aliases,
        compiler_params=params(1),
        cost_estimate=cost(),
        name="high_level",
    )(*operands, *after)


def local(fourier, order_slot, coeff_self, coeff_pair):
    fourier = pltpu.with_memory_space_constraint(fourier, pltpu.HBM)
    order_count = lax.axis_size("order")
    level_count = lax.axis_size("level")
    levels, orders_here, blocks_here, cycle_rows, _ = coeff_self.shape
    rows_here, columns = fourier.shape[3:]
    local_bits = blocks_here.bit_length() - 1
    steps = levels - local_bits
    group = blocks_here // level_count
    parts, pieces, modes, order = plan(orders_here, steps, rows_here % 16 == 0)
    quarter = columns // 4
    chunks = [(slot, first * quarter, count * quarter) for slot, first, count in parts]

    def place(axis):
        return lax.axis_index(axis).astype(jnp.int32).reshape(1)

    places = (place("level"), place("order"), order_slot)
    level_masks = tuple(range(1, level_count))
    shape = (orders_here, blocks_here, cycle_rows, columns)
    where = [
        (at, slot, start + piece * (width // count), width // count)
        for at, ((slot, start, width), count) in enumerate(zip(chunks, pieces))
        for piece in range(count)
    ]
    outgoing, rows, state = {}, {}, {}
    result = None
    last = []
    for kind, at in order:
        if kind in (TAKE, GATHER, LOW):
            chunk, mode = chunks[at], modes[at]
            slot, start, width = chunk
        if kind == TAKE:
            masks = () if mode == DIRECT else level_masks
            outgoing[at] = take_rows(fourier, places, chunk, masks, order_count, last)
            last = [outgoing[at][0]]
            if mode == DIRECT:
                value = outgoing[at][0].reshape(
                    order_count * level_count, group, rows_here, width
                )
                value = lax.all_to_all(
                    value, ("order", "level"), split_axis=0, concat_axis=0, tiled=True
                )
                value = value.reshape(order_count, level_count, group, rows_here, width)
                if rows_here % 16:
                    value = value.transpose(1, 2, 0, 3, 4).reshape(
                        1, level_count, group, cycle_rows, width
                    )
                rows[at] = [value]
        elif kind == GATHER:
            received = [swap(value, "level", mask) for value, mask in zip(outgoing[at], level_masks)]
            gathered = gather_blocks(
                fourier, received, places, chunk, order_count, mode == PAIRS, last
            )
            last = [gathered[0]]
            if mode == PAIRS:
                rows[at] = [gathered[0]] + [
                    swap(value, "order", mask) for mask, value in enumerate(gathered) if mask
                ]
            else:
                rows[at] = [
                    lax.all_to_all(gathered[0], "order", split_axis=0, concat_axis=0, tiled=True)
                ]
        elif kind == LOW:
            lowest = low_levels(
                rows[at],
                places[1],
                coeff_self,
                coeff_pair,
                slot,
                mode == DIRECT,
                pieces[at],
                last,
            )
            last = [lowest[0]]
            first = [piece for piece, (chunk, *_) in enumerate(where) if chunk == at][0]
            state.update(enumerate(lowest, first))
        else:
            _, slot, start, width = where[at]
            other = swap(state[at], "level", 1 << (kind - 1))
            final = None
            if kind == steps:
                final = (result, shape, start // width)
                last = [value for value in last if value is not result]
            state[at] = high_level(
                state[at], other, coeff_self, coeff_pair, local_bits + kind - 1, slot, last, final
            )
            last = [state[at]]
            if kind == steps:
                result = state[at]
    return result


def solution(mesh):
    placed = (
        P("freq", None, "level", "order", None),
        P(),
        P(None, "order", "level", None, None),
        P(None, "order", "level", None, None),
    )
    return jax.shard_map(
        local,
        mesh=mesh,
        in_specs=placed,
        out_specs=P(("freq", "order"), "level", None, None),
        check_vma=False,
    )
```

```python
import functools

import jax
import jax.numpy as jnp
from jax import lax
from jax.experimental import pallas as pl
from jax.experimental.pallas import tpu as pltpu
from jax.sharding import PartitionSpec as P

VMEM = 48 * 1024 * 1024
TAKE, GATHER, LOW = "take", "gather", "low"
DIRECT, MIXED, PAIRS = "direct", "mixed", "pairs"
CHUNKS = ((0, 0, 2), (0, 2, 2), (1, 0, 2), (1, 2, 2))
PIECES = (1, 1, 1, 1,)
MODES = (DIRECT, DIRECT, DIRECT, MIXED)
ORDER = (
    (TAKE, 0), (TAKE, 1), (LOW, 0), (TAKE, 3), (TAKE, 2), (1, 0), (LOW, 1), (1, 1), (LOW, 2),
    (GATHER, 3), (2, 0), (1, 2), (LOW, 3), (2, 1), (1, 3), (2, 2), (2, 3),
)


def plan(slots, steps, pairs):
    if steps == 2 and pairs and slots == 1 + max(slot for slot, _, _ in CHUNKS):
        return CHUNKS, PIECES, MODES, ORDER
    chunks = [(slot, part, 2) for slot in range(slots) for part in (0, 2)]
    count = len(chunks)
    order = []
    for turn in range(count + steps + 2):
        jobs = [(TAKE, turn), (LOW, turn - 1)]
        jobs += [(step, turn - 1 - step) for step in range(1, steps + 1)]
        order += [job for job in jobs if 0 <= job[1] < count]
    return chunks, (1,) * count, (DIRECT,) * count, order


def params(steps):
    return pltpu.CompilerParams(
        dimension_semantics=("arbitrary",) * steps, vmem_limit_bytes=VMEM
    )


def cost():
    return pl.CostEstimate(flops=0, bytes_accessed=1024, transcendentals=0)


def anywhere(values):
    return [pl.BlockSpec(memory_space=pl.ANY)] * len(values)


def swap(value, axis, mask):
    pairs = [(source, source ^ mask) for source in range(lax.axis_size(axis))]
    return lax.ppermute(value, axis, pairs)


def copy_kernel(count, level_ref, order_ref, slot_ref, *refs):
    for source, target in zip(refs[:count], refs[-count:]):
        target[...] = source[...].reshape(target.shape)


def take_rows(fourier, places, chunk, masks, order_count, after):
    slot, start, width = chunk
    _, blocks, _, rows, _ = fourier.shape
    slots_here = places[2].shape[0] // order_count
    group = blocks // lax.axis_size("level") if masks else blocks

    def source_map(mask, order, level, coordinate, slots):
        part = level[0] ^ mask if masks else 0
        return (slots[order * slots_here + slot], part, 0, 0, start // width)

    shape = (order_count, group, rows, width)
    return pl.pallas_call(
        functools.partial(copy_kernel, len(masks) or 1),
        grid_spec=pltpu.PrefetchScalarGridSpec(
            num_scalar_prefetch=3,
            grid=(order_count,),
            in_specs=[
                pl.BlockSpec((1, group, 1, rows, width), functools.partial(source_map, mask))
                for mask in masks or (0,)
            ]
            + anywhere(after),
            out_specs=[
                pl.BlockSpec((1,) + shape[1:], lambda order, *places: (order, 0, 0, 0))
                for _ in masks or (0,)
            ],
        ),
        out_shape=[jax.ShapeDtypeStruct(shape, fourier.dtype) for _ in masks or (0,)],
        compiler_params=params(1),
        cost_estimate=cost(),
        name="take_rows",
    )(*places, *[fourier] * (len(masks) or 1), *after)


def gather_kernel(sources, targets, level_ref, order_ref, slot_ref, *refs):
    for index, target in enumerate(refs[-targets:]):

        @pl.when((pl.program_id(0) == index) | (targets == 1))
        def _(target=target):
            for mask, source in enumerate(refs[:sources]):
                at = level_ref[0] ^ mask
                place = target.at[0, :, pl.ds(at, 1)] if targets == 1 else target.at[:, pl.ds(at, 1)]
                place[...] = source[...].reshape(place.shape)


def gather_blocks(fourier, received, places, chunk, order_count, apart, after):
    slot, start, width = chunk
    _, blocks, _, rows, _ = fourier.shape
    slots_here = places[2].shape[0] // order_count
    level_count = lax.axis_size("level")
    group = blocks // level_count

    def order_at(step, coordinate):
        return coordinate[0] ^ step if apart else step

    def own_map(step, level, coordinate, slots):
        order = order_at(step, coordinate)
        return (slots[order * slots_here + slot], level[0], 0, 0, start // width)

    def received_map(step, level, coordinate, slots):
        return (order_at(step, coordinate), 0, 0, 0)

    shape = (group, level_count, rows, width)
    if apart:
        out_specs = [pl.BlockSpec(shape, lambda step, *places: (0, 0, 0, 0))] * order_count
        out_shape = [jax.ShapeDtypeStruct(shape, fourier.dtype)] * order_count
    else:
        out_specs = [pl.BlockSpec((1,) + shape, lambda step, *places: (step, 0, 0, 0, 0))]
        out_shape = [jax.ShapeDtypeStruct((order_count,) + shape, fourier.dtype)]
    return pl.pallas_call(
        functools.partial(gather_kernel, level_count, len(out_shape)),
        grid_spec=pltpu.PrefetchScalarGridSpec(
            num_scalar_prefetch=3,
            grid=(order_count,),
            in_specs=[pl.BlockSpec((1, group, 1, rows, width), own_map)]
            + [pl.BlockSpec((1, group, rows, width), received_map) for _ in received]
            + anywhere(after),
            out_specs=out_specs,
        ),
        out_shape=out_shape,
        compiler_params=params(1),
        cost_estimate=cost(),
        name="gather_blocks",
    )(*places, fourier, *received, *after)


def low_kernel(source_first, count, pieces, order_ref, *refs):
    rows_refs, (self_ref, pair_ref) = refs[:count], refs[count : count + 2]
    out_refs, state = refs[-2 - pieces : -2], refs[-2]
    rows_ref = refs[-1] if count > 1 else rows_refs[0]
    level = pl.program_id(0)
    blocks = state.shape[0]
    bits = blocks.bit_length() - 1
    fold = self_ref.shape[0]
    groups, first, second = rows_ref.shape[:3]

    def block_of(height, block):
        if height:
            return [state[block]]
        if source_first:
            at = (block % first, block // first)
        else:
            at = (block // second, block % second)
        return [rows_ref[(group,) + at] for group in range(groups)]

    for height in range(bits):

        @pl.when(level == height // fold)
        def _(height=height):
            if height == 0 and count > 1:
                for mask, source in enumerate(rows_refs):
                    rows_ref[pl.ds(order_ref[0] ^ mask, 1)] = source[...].reshape(
                        (1,) + source.shape
                    )
            targets = out_refs if height == bits - 1 else (state,)
            at = height % fold
            for low in range(blocks):
                high = low ^ (1 << height)
                if high < low:
                    continue
                values = jnp.concatenate(block_of(height, low) + block_of(height, high), axis=0)
                factors = jnp.concatenate(
                    [
                        jnp.concatenate([self_ref[at, 0, low], pair_ref[at, 0, low]], axis=1),
                        jnp.concatenate([pair_ref[at, 0, high], self_ref[at, 0, high]], axis=1),
                    ],
                    axis=0,
                )
                mixed = jnp.dot(factors, values, preferred_element_type=jnp.float32)
                mixed = mixed.astype(state.dtype)
                half, width = mixed.shape[0] // 2, mixed.shape[1] // len(targets)
                for piece, target in enumerate(targets):
                    columns = slice(piece * width, (piece + 1) * width)
                    target[low] = mixed[:half, columns]
                    target[high] = mixed[half:, columns]


def low_levels(rows, order, coeff_self, coeff_pair, slot, source_first, pieces, after):
    rows = [pltpu.with_memory_space_constraint(value, pltpu.HBM) for value in rows]
    width = rows[0].shape[-1]
    blocks, cycle = coeff_self.shape[2:4]
    bits = blocks.bit_length() - 1
    shape = (blocks, cycle, width // pieces)
    fold = 2 if bits % 2 == 0 else 1
    factor = pl.BlockSpec(
        (fold, 1, blocks, cycle, cycle), lambda level, *order: (level, slot, 0, 0, 0)
    )
    scratch = [pltpu.VMEM((blocks, cycle, width), rows[0].dtype)]
    scratch.append(
        pltpu.VMEM((len(rows),) + rows[0].shape if len(rows) > 1 else (8, 128), rows[0].dtype)
    )
    return pl.pallas_call(
        functools.partial(low_kernel, source_first, len(rows), pieces),
        grid_spec=pltpu.PrefetchScalarGridSpec(
            num_scalar_prefetch=1,
            grid=(bits // fold,),
            in_specs=[
                pl.BlockSpec(value.shape, lambda level, *order, rank=value.ndim: (0,) * rank)
                for value in rows
            ]
            + [factor, factor]
            + anywhere(after),
            out_specs=[pl.BlockSpec(shape, lambda level, *order: (0, 0, 0))] * pieces,
            scratch_shapes=scratch,
        ),
        out_shape=[jax.ShapeDtypeStruct(shape, rows[0].dtype)] * pieces,
        compiler_params=params(1),
        cost_estimate=cost(),
        name="low_levels",
    )(order, *rows, coeff_self, coeff_pair, *after)


def high_kernel(own_ref, other_ref, self_ref, pair_ref, *refs):
    target = refs[-1]
    lead = len(target.shape) - 3
    for block in range(own_ref.shape[0]):
        factors = jnp.concatenate([self_ref[0, 0, block], pair_ref[0, 0, block]], axis=1)
        values = jnp.concatenate([own_ref[block], other_ref[block]], axis=0)
        mixed = jnp.dot(factors, values, preferred_element_type=jnp.float32)
        target[(0,) * lead + (block,)] = mixed.astype(target.dtype)


def high_level(own, other, coeff_self, coeff_pair, level, slot, after, final=None):
    blocks, cycle, width = own.shape
    step = min(8, blocks)
    value = pl.BlockSpec((step, cycle, width), lambda at: (at, 0, 0))
    factor = pl.BlockSpec((1, 1, step, cycle, cycle), lambda at: (level, slot, at, 0, 0))
    operands = [own, other, coeff_self, coeff_pair]
    in_specs = [value, value, factor, factor]
    aliases = {}
    if final is None:
        out_spec, out_shape = value, jax.ShapeDtypeStruct(own.shape, own.dtype)
    else:
        result, shape, part = final
        out_spec = pl.BlockSpec((1, step, cycle, width), lambda at: (slot, at, 0, part))
        out_shape = jax.ShapeDtypeStruct(shape, own.dtype)
        if result is not None:
            operands.append(result)
            in_specs += anywhere([result])
            aliases = {4: 0}
    return pl.pallas_call(
        high_kernel,
        grid=(blocks // step,),
        in_specs=in_specs + anywhere(after),
        out_specs=out_spec,
        out_shape=out_shape,
        input_output_aliases=aliases,
        compiler_params=params(1),
        cost_estimate=cost(),
        name="high_level",
    )(*operands, *after)


def local(fourier, order_slot, coeff_self, coeff_pair):
    fourier = pltpu.with_memory_space_constraint(fourier, pltpu.HBM)
    order_count = lax.axis_size("order")
    level_count = lax.axis_size("level")
    levels, orders_here, blocks_here, cycle_rows, _ = coeff_self.shape
    rows_here, columns = fourier.shape[3:]
    local_bits = blocks_here.bit_length() - 1
    steps = levels - local_bits
    group = blocks_here // level_count
    parts, pieces, modes, order = plan(orders_here, steps, rows_here % 16 == 0)
    quarter = columns // 4
    chunks = [(slot, first * quarter, count * quarter) for slot, first, count in parts]

    def place(axis):
        return lax.axis_index(axis).astype(jnp.int32).reshape(1)

    places = (place("level"), place("order"), order_slot)
    level_masks = tuple(range(1, level_count))
    shape = (orders_here, blocks_here, cycle_rows, columns)
    where = [
        (at, slot, start + piece * (width // count), width // count)
        for at, ((slot, start, width), count) in enumerate(zip(chunks, pieces))
        for piece in range(count)
    ]
    outgoing, rows, state = {}, {}, {}
    result = None
    last = []
    for kind, at in order:
        if kind in (TAKE, GATHER, LOW):
            chunk, mode = chunks[at], modes[at]
            slot, start, width = chunk
        if kind == TAKE:
            masks = () if mode == DIRECT else level_masks
            outgoing[at] = take_rows(fourier, places, chunk, masks, order_count, last)
            last = [outgoing[at][0]]
            if mode == DIRECT:
                value = outgoing[at][0].reshape(
                    order_count * level_count, group, rows_here, width
                )
                value = lax.all_to_all(
                    value, ("order", "level"), split_axis=0, concat_axis=0, tiled=True
                )
                value = value.reshape(order_count, level_count, group, rows_here, width)
                if rows_here % 16:
                    value = value.transpose(1, 2, 0, 3, 4).reshape(
                        1, level_count, group, cycle_rows, width
                    )
                rows[at] = [value]
        elif kind == GATHER:
            received = [swap(value, "level", mask) for value, mask in zip(outgoing[at], level_masks)]
            gathered = gather_blocks(
                fourier, received, places, chunk, order_count, mode == PAIRS, last
            )
            last = [gathered[0]]
            if mode == PAIRS:
                rows[at] = [gathered[0]] + [
                    swap(value, "order", mask) for mask, value in enumerate(gathered) if mask
                ]
            else:
                rows[at] = [
                    lax.all_to_all(gathered[0], "order", split_axis=0, concat_axis=0, tiled=True)
                ]
        elif kind == LOW:
            lowest = low_levels(
                rows[at],
                places[1],
                coeff_self,
                coeff_pair,
                slot,
                mode == DIRECT,
                pieces[at],
                last,
            )
            last = [lowest[0]]
            first = [piece for piece, (chunk, *_) in enumerate(where) if chunk == at][0]
            state.update(enumerate(lowest, first))
        else:
            _, slot, start, width = where[at]
            other = swap(state[at], "level", 1 << (kind - 1))
            final = None
            if kind == steps:
                final = (result, shape, start // width)
                last = [value for value in last if value is not result]
            state[at] = high_level(
                state[at], other, coeff_self, coeff_pair, local_bits + kind - 1, slot, last, final
            )
            last = [state[at]]
            if kind == steps:
                result = state[at]
    return result


def solution(mesh):
    placed = (
        P("freq", None, "level", "order", None),
        P(),
        P(None, "order", "level", None, None),
        P(None, "order", "level", None, None),
    )
    return jax.shard_map(
        local,
        mesh=mesh,
        in_specs=placed,
        out_specs=P(("freq", "order"), "level", None, None),
        check_vma=False,
    )
```
